32 devices in a mesh: aux: 32 (over z, y, x, core).
Axes of the slice: x: 2, y: 2, z: 4, core: 2. Of those that a mesh axis runs over, the one named last changes fastest.
Arguments:
- rho_real: float32 [64, 256, 256], P('aux'), may hold values from -6 to 6
- rho_imag: float32 [64, 256, 256], P('aux'), may hold values from -6 to 6
- hamiltonian: float32 [256, 256], replicated, may hold values from -0.375 to 0.375
- damping: float32 [256], replicated, may hold values from 0.5 to 4
- up_scale: float32 [256], replicated, may hold values from 0.2 to 1
- bath_real: float32 [256], replicated, may hold values from 0.1 to 1
- bath_imag: float32 [256], replicated, may hold values from -1 to -0.1
- link_neighbor: int32 [64, 64], P('aux'), may hold values from 0 to 63, as said below
- link_site: int32 [64, 64], P('aux'), may hold values from 0 to 255, as said below
- link_occupation: int32 [64, 64], P('aux'), may hold values from 0 to 2, as said below
Outputs:
- next_real: float32 [64, 256, 256], P('aux')
- next_imag: float32 [64, 256, 256], P('aux')
The draws below stay inside these ranges and needn't reach their ends.
Inputs may be any that keep to these rules, and one draw needn't show every extreme that they name: `link_neighbor`: matrix m is held by device m // 2. Of the links of one device's matrices, at most 8 name matrices held by any one device, and in every draw exactly 8 do for some pair of devices. `link_site`: the 64 sites of one matrix are distinct. `link_occupation`: links to higher tiers have occupation 1. The last 3 links of a matrix hold its own occupations, which sum to 1 or 2; a zero marks an unoccupied site.
All inputs are finite; a program needn't handle non-finite values.
Results may differ from the reference program's by a relative error of at most 0.0001.
Values sent between devices are 32-bit elements; how exact they have to be, the bound alone decides.
A program may use at most 64 MiB of HBM per device.

```python
import math
import jax
import jax.numpy as jnp
from jax import lax

SITES = 256
MAT_DEV = 2
DOWN = 3
LINKS = 64
MATS = 64
CAP = 8
N_AUX = 32


def draw_link_neighbor(key, part):
    key = jax.random.fold_in(key, 11)
    flat_links = MAT_DEV * LINKS

    def for_device(dev_key):
        key_hot, key_order, key_shuffle, key_local = jax.random.split(dev_key, 4)
        hottest = jax.random.randint(key_hot, (), 0, N_AUX)
        owner_pool = jnp.arange(N_AUX * CAP, dtype=jnp.int32) // CAP
        scores = jax.random.permutation(key_order, N_AUX * CAP).astype(jnp.int32)
        ranked = jnp.where(owner_pool == hottest, -1, scores)
        ordering = jnp.argsort(ranked, stable=True)
        chosen = owner_pool[ordering[:flat_links]]
        owners = jax.random.permutation(key_shuffle, chosen)
        local_index = jax.random.randint(key_local, (flat_links,), 0, MAT_DEV)
        return owners * MAT_DEV + local_index
    device_keys = jax.random.split(key, N_AUX)
    return jax.vmap(for_device)(device_keys).reshape(MATS, LINKS).astype(jnp.int32)


def draw_link_site(key, part):
    key = jax.random.fold_in(key, 23)
    matrix_keys = jax.random.split(key, MATS)

    def for_matrix(mat_key):
        return jax.random.permutation(mat_key, SITES)[:LINKS]
    return jax.vmap(for_matrix)(matrix_keys).astype(jnp.int32)


def draw_link_occupation(key, part):
    key = jax.random.fold_in(key, 37)
    patterns = jnp.array([[1, 0, 0], [2, 0, 0], [1, 1, 0]], dtype=jnp.int32)
    matrix_keys = jax.random.split(key, MATS)

    def for_matrix(mat_key):
        key_pick, key_perm = jax.random.split(mat_key)
        chosen = patterns[jax.random.randint(key_pick, (), 0, 3)]
        own = jax.random.permutation(key_perm, chosen)
        return jnp.concatenate([jnp.ones((LINKS - DOWN,), jnp.int32), own])
    return jax.vmap(for_matrix)(matrix_keys).astype(jnp.int32)


def block_scale(own_key, extent, cuts, smallest, largest):
    def one(axis_at, parts):
        draws = jax.random.uniform(jax.random.fold_in(jax.random.fold_in(own_key, 6), axis_at), (parts,), jnp.float32, smallest / len(cuts), largest / len(cuts))
        return jnp.repeat(jnp.exp(draws), extent[axis_at] // parts).reshape((-1,) + (1,) * (len(extent) - axis_at - 1))

    factor_of = one(*cuts[0])
    for cut in cuts[1:]:
        factor_of = factor_of * one(*cut)
    return factor_of


def centred(stream_key, dims, scale, most, cuts=(), kind=jnp.bfloat16):
    drawn = scale * jax.random.normal(stream_key, dims, jnp.float32)
    if cuts:
        drawn = drawn * block_scale(stream_key, dims, cuts, -0.22, 0.18)
    return jnp.clip(drawn, -most, most).astype(kind)


def setup_inputs(seed: int = 0) -> dict:
    key_list = jax.random.split(jax.random.key(seed), 11)
    rho_real = centred(key_list[0], (MATS, SITES, SITES), 1.0, 6.0, ((0, 32),), jnp.float32)
    rho_imag = centred(key_list[1], (MATS, SITES, SITES), 1.0, 6.0, ((0, 32),), jnp.float32)
    hamiltonian = centred(key_list[2], (SITES, SITES), SITES ** -0.5, 0.375, (), jnp.float32)
    damping = jnp.clip(jnp.exp(jax.random.uniform(key_list[3], (SITES,), jnp.float32, math.log(0.5), math.log(4.0))), 0.5, 4.0)
    up_scale = jnp.clip(jnp.exp(jax.random.uniform(key_list[4], (SITES,), jnp.float32, math.log(0.2), math.log(1.0))), 0.2, 1.0)
    bath_real = jnp.clip(jax.random.uniform(key_list[5], (SITES,), jnp.float32, 0.1, 1.0), 0.1, 1.0)
    bath_imag = jnp.clip(jax.random.uniform(key_list[6], (SITES,), jnp.float32, -1.0, -0.1), -1.0, -0.1)
    link_neighbor = draw_link_neighbor(jax.random.fold_in(key_list[10], 71), 0)
    link_site = draw_link_site(jax.random.fold_in(key_list[10], 71), 0)
    link_occupation = draw_link_occupation(jax.random.fold_in(key_list[10], 71), 0)
    return {"rho_real": rho_real, "rho_imag": rho_imag, "hamiltonian": hamiltonian, "damping": damping, "up_scale": up_scale, "bath_real": bath_real, "bath_imag": bath_imag, "link_neighbor": link_neighbor, "link_site": link_site, "link_occupation": link_occupation}


STEP_SIZE = 0.25

def coefficients(scale_up, bath_re, bath_im, occupation):
    occupied = occupation.astype(jnp.float32)
    upward = jnp.arange(occupation.shape[1]) < occupation.shape[1] - DOWN
    strength = scale_up * jnp.sqrt(occupied)
    row_real = jnp.where(upward, 0.0, occupied * bath_im)
    row_imag = jnp.where(upward, -strength, -occupied * bath_re)
    col_real = jnp.where(upward, 0.0, occupied * bath_im)
    col_imag = jnp.where(upward, strength, occupied * bath_re)
    return (row_real, row_imag, col_real, col_imag)

def local_slope(state_re, state_im, hamilton, damping, pieces, link_coef, onehot):
    highest = lax.Precision.HIGHEST
    comm_re = jnp.matmul(hamilton, state_re, precision=highest) - jnp.matmul(state_re, hamilton, precision=highest)
    comm_im = jnp.matmul(hamilton, state_im, precision=highest) - jnp.matmul(state_im, hamilton, precision=highest)
    row_real, row_imag, col_real, col_imag = link_coef
    rowx_re = pieces[:, :, 0]
    rowx_im = pieces[:, :, 1]
    colx_re = pieces[:, :, 2]
    colx_im = pieces[:, :, 3]
    rowterm_re = row_real[:, :, None] * rowx_re - row_imag[:, :, None] * rowx_im
    rowterm_im = row_real[:, :, None] * rowx_im + row_imag[:, :, None] * rowx_re
    colterm_re = col_real[:, :, None] * colx_re - col_imag[:, :, None] * colx_im
    colterm_im = col_real[:, :, None] * colx_im + col_imag[:, :, None] * colx_re
    added_re = jnp.einsum('mla,mlb->mab', onehot, rowterm_re, precision=highest) + jnp.einsum('mla,mlb->mab', colterm_re, onehot, precision=highest)
    added_im = jnp.einsum('mla,mlb->mab', onehot, rowterm_im, precision=highest) + jnp.einsum('mla,mlb->mab', colterm_im, onehot, precision=highest)
    out_re = comm_im - damping[:, None, None] * state_re + added_re
    out_im = -comm_re - damping[:, None, None] * state_im + added_im
    return (out_re, out_im)

def reference(rho_real, rho_imag, hamiltonian, damping, up_scale, bath_real, bath_imag, link_neighbor, link_site, link_occupation):
    hamilton = 0.5 * (hamiltonian + hamiltonian.T)
    link_coef = coefficients(up_scale[link_site], bath_real[link_site], bath_imag[link_site], link_occupation)
    downward = jnp.arange(LINKS) >= LINKS - DOWN
    gamma = lax.optimization_barrier(jnp.sum(jnp.where(downward[None, :], link_occupation.astype(jnp.float32) * damping[link_site], 0.0), axis=1))
    onehot = (link_site[:, :, None] == jnp.arange(SITES, dtype=jnp.int32)[None, None, :]).astype(jnp.float32)

    def slope(state_re, state_im):
        pieces = jnp.stack([state_re[link_neighbor, link_site, :], state_im[link_neighbor, link_site, :], state_re[link_neighbor, :, link_site], state_im[link_neighbor, :, link_site]], axis=2)
        members = (state_re, state_im, gamma, pieces) + tuple(link_coef) + (onehot,)
        grouped = tuple((member.reshape((N_AUX, MAT_DEV) + member.shape[1:]) for member in members))

        def blockwise(items):
            return local_slope(items[0], items[1], hamilton, items[2], items[3], items[4:8], items[8])
        out_re, out_im = lax.map(blockwise, grouped)
        return (out_re.reshape(state_re.shape), out_im.reshape(state_im.shape))
    slope_re, slope_im = slope(rho_real, rho_imag)
    total_re, total_im = (slope_re, slope_im)
    for weight, factor in zip((0.5 * STEP_SIZE, 0.5 * STEP_SIZE, STEP_SIZE), (2.0, 2.0, 1.0)):
        section_re = rho_real + weight * slope_re
        section_im = rho_imag + weight * slope_im
        slope_re, slope_im = slope(section_re, section_im)
        total_re = total_re + factor * slope_re
        total_im = total_im + factor * slope_im
    return (rho_real + STEP_SIZE / 6.0 * total_re, rho_imag + STEP_SIZE / 6.0 * total_im)
```

```python
import functools

import jax
import jax.numpy as jnp
from jax import lax
from jax.experimental import pallas as pl
from jax.experimental.pallas import tpu as pltpu
from jax.sharding import PartitionSpec as P

DOWN = 3
STEP_SIZE = 0.25
MESH = pl.DeviceIdType.MESH
F32 = jnp.float32
BF16 = jnp.bfloat16
NN = (((1,), (0,)), ((), ()))
NT = (((1,), (1,)), ((), ()))


def split(value):
    high = value.astype(BF16)
    return high, (value - high.astype(F32)).astype(BF16)


def dot(a, b, dims=NN):
    return lax.dot_general(a, b, dims, preferred_element_type=F32)


def exact_dot(a, b):
    return jnp.dot(a, b, precision=lax.Precision.HIGHEST, preferred_element_type=F32)


def kernel(
    peers,
    cap,
    mat_dev,
    link_count,
    sites,
    rho_re,
    rho_im,
    ham_in,
    damping,
    up_scale,
    bath_re,
    bath_im,
    table,
    cur_re,
    cur_im,
    send,
    recv,
    req_send,
    req_recv,
    ham,
    acc,
    base,
    pick,
    put,
    coef_re,
    coef_im,
    stack,
    wide,
    terms,
    req_sems,
    send_sems,
    recv_sems,
):
    me = lax.axis_index("aux")
    slots = peers * cap
    links = mat_dev * link_count

    barrier = pltpu.get_barrier_semaphore()

    def greet(k, carry):
        pl.semaphore_signal(
            barrier, inc=1, device_id=(lax.rem(me + k, peers),), device_id_type=MESH
        )
        return carry

    lax.fori_loop(1, peers, greet, 0)

    neighbor = table[0:1, :]
    site = table[1:2, :]
    occupied = table[2:3, :]
    owner = neighbor // mat_dev
    owner_here = jnp.broadcast_to(owner.astype(F32), (links, links))
    owner_there = owner_here.T
    first = lax.broadcasted_iota(jnp.int32, (links, links), 0)
    second = lax.broadcasted_iota(jnp.int32, (links, links), 1)
    earlier = jnp.where((owner_here == owner_there) & (first < second), 1.0, 0.0)
    rank = jnp.sum(earlier, axis=0, keepdims=True).astype(jnp.int32)
    slot = owner * cap + rank
    lane = lax.broadcasted_iota(jnp.int32, (1, links), 1)
    holder = lane // link_count
    upward = (lane - holder * link_count < link_count - DOWN).astype(jnp.int32)
    code = site + sites * (
        (neighbor - owner * mat_dev) + mat_dev * (holder + mat_dev * (upward + 2 * occupied))
    )
    slot_index = lax.broadcasted_iota(jnp.int32, (slots, links), 0)
    code_slot = (
        jnp.sum(
            jnp.where(slot_index == slot, (code + 1).astype(F32), 0.0), axis=1, keepdims=True
        ).astype(jnp.int32)
        - 1
    )
    used = code_slot >= 0
    safe = jnp.maximum(code_slot, 0)
    wanted = jnp.where(used, safe % (sites * mat_dev), -1)
    req_send[...] = jnp.broadcast_to(wanted, (slots, 128)).reshape(peers, cap, 128)

    pl.semaphore_wait(barrier, peers - 1)

    def request(k, carry):
        peer = lax.rem(me + k, peers)
        pltpu.make_async_remote_copy(
            src_ref=req_send.at[peer],
            dst_ref=req_recv.at[me],
            send_sem=req_sems.at[0],
            recv_sem=req_sems.at[1],
            device_id=(peer,),
            device_id_type=MESH,
        ).start()
        return carry

    lax.fori_loop(1, peers, request, 0)
    req_recv[me] = req_send[me]

    site_slot = jnp.where(used, safe % sites, -1)
    rest = safe // (sites * mat_dev)
    holder_slot = jnp.where(used, rest % mat_dev, -1)
    rest = rest // mat_dev
    up_slot = used & (rest % 2 == 1)
    occ_slot = jnp.where(used, (rest // 2).astype(F32), 0.0)
    own_site = lax.broadcasted_iota(jnp.int32, (slots, sites), 1) == site_slot

    def look_up(ref):
        return jnp.sum(jnp.where(own_site, ref[...], 0.0), axis=1, keepdims=True)

    part_re = jnp.where(up_slot, 0.0, occ_slot * look_up(bath_im))
    part_im = jnp.where(up_slot, look_up(up_scale) * jnp.sqrt(occ_slot), occ_slot * look_up(bath_re))
    coef_re[...] = jnp.broadcast_to(part_re, (slots, sites))
    coef_im[...] = jnp.broadcast_to(part_im, (slots, sites))
    rate = jnp.where(up_slot, 0.0, occ_slot * look_up(damping))
    gamma = [
        jnp.sum(jnp.where(holder_slot == m, rate, 0.0), axis=0, keepdims=True)
        for m in range(mat_dev)
    ]
    target = jnp.where(used, holder_slot * sites + site_slot, -1).astype(F32)
    target = jnp.broadcast_to(target, (slots, 128)).T[0:1, :].astype(jnp.int32)
    placed = lax.broadcasted_iota(jnp.int32, (mat_dev * sites, slots), 0) == target
    placed = jnp.where(placed, 1.0, 0.0).astype(BF16)
    put[:, 0:slots] = placed
    put[:, slots:] = placed

    ham[...] = 0.5 * (ham_in[...] + ham_in[...].T)
    cur_re[...] = rho_re[...]
    cur_im[...] = rho_im[...]
    acc[...] = jnp.zeros_like(acc)

    pltpu.make_async_copy(
        req_recv.at[pl.ds(0, peers - 1)], req_recv.at[pl.ds(0, peers - 1)], req_sems.at[1]
    ).wait()
    asked = req_recv[...].reshape(slots, 128)[:, 0:1]
    depth = mat_dev * sites
    picked = lax.broadcasted_iota(jnp.int32, (slots, depth), 1) == asked
    picked = jnp.where(picked, 1.0, 0.0).astype(BF16)
    pick[:, 0:depth] = picked
    pick[:, depth:] = picked

    def stage(t, carry):
        for c, cur in enumerate((cur_re, cur_im)):
            for m in range(mat_dev):
                high, low = split(cur[m])
                stack[c, m * sites : (m + 1) * sites, :] = high
                stack[c, depth + m * sites : depth + (m + 1) * sites, :] = low
                wide[c, :, m * sites : (m + 1) * sites] = high
                wide[c, :, depth + m * sites : depth + (m + 1) * sites] = low
        for c in range(2):
            send[t, :, c] = dot(pick[...], stack[c]).reshape(peers, cap, sites)
            send[t, :, 2 + c] = dot(pick[...], wide[c], NT).reshape(peers, cap, sites)

        def post(k, carry):
            peer = lax.rem(me + k, peers)
            pltpu.make_async_remote_copy(
                src_ref=send.at[t, peer],
                dst_ref=recv.at[t, me],
                send_sem=send_sems.at[t],
                recv_sem=recv_sems.at[t],
                device_id=(peer,),
                device_id_type=MESH,
            ).start()
            return carry

        lax.fori_loop(peers // 2, peers, post, 0)
        lax.fori_loop(1, peers // 2, post, 0)
        recv[t, me] = send[t, me]

        last = t == 3
        weight = jnp.where(last, STEP_SIZE / 6.0, jnp.where(t == 2, STEP_SIZE, 0.5 * STEP_SIZE))
        share = jnp.where(t == 0, -1.0 / 3.0, jnp.where(t == 2, 2.0 / 3.0, 1.0 / 3.0))
        keep = jnp.where(last, 0.0, 1.0)
        for m in range(mat_dev):
            here_re, here_im = cur_re[m], cur_im[m]
            acc_re = acc[m, 0] + share * here_re
            acc_im = acc[m, 1] + share * here_im
            acc[m, 0] = acc_re
            acc[m, 1] = acc_im
            comm_re = exact_dot(ham[...], here_re) - exact_dot(here_re, ham[...])
            comm_im = exact_dot(ham[...], here_im) - exact_dot(here_im, ham[...])
            from_re = jnp.where(last, acc_re, rho_re[m])
            from_im = jnp.where(last, acc_im, rho_im[m])
            base[m, 0] = from_re + weight * (comm_im - gamma[m] * here_re)
            base[m, 1] = from_im - weight * (comm_re + gamma[m] * here_im)

        pltpu.make_async_copy(
            recv.at[t, pl.ds(0, peers - 1)], recv.at[t, pl.ds(0, peers - 1)], recv_sems.at[t]
        ).wait()
        pieces = [recv[t, :, q].reshape(slots, sites) for q in range(4)]
        by_re = weight * coef_re[...]
        by_im = weight * coef_im[...]
        added = []
        for q, term in enumerate(
            (
                by_re * pieces[0] + by_im * pieces[1],
                by_re * pieces[1] - by_im * pieces[0],
                by_re * pieces[2] - by_im * pieces[3],
                by_re * pieces[3] + by_im * pieces[2],
            )
        ):
            high, low = split(term)
            terms[q, 0:slots, :] = high
            terms[q, slots:, :] = low
            added.append(dot(put[...], terms[q]))
        for c, cur in enumerate((cur_re, cur_im)):
            for m in range(mat_dev):
                rows = slice(m * sites, (m + 1) * sites)
                cur[m] = base[m, c] + added[c][rows] + added[2 + c][rows].T
        return carry

    lax.fori_loop(0, 4, stage, 0)

    pltpu.make_async_copy(
        req_send.at[pl.ds(0, peers - 1)], req_send.at[pl.ds(0, peers - 1)], req_sems.at[0]
    ).wait()
    for t in range(4):
        pltpu.make_async_copy(
            send.at[t, pl.ds(0, peers - 1)], send.at[t, pl.ds(0, peers - 1)], send_sems.at[t]
        ).wait()


def local(
    rho_real,
    rho_imag,
    hamiltonian,
    damping,
    up_scale,
    bath_real,
    bath_imag,
    link_neighbor,
    link_site,
    link_occupation,
):
    peers = lax.axis_size("aux")
    mat_dev, link_count = link_neighbor.shape
    sites = rho_real.shape[1]
    links = mat_dev * link_count
    cap = -(-max(2, 2 * links // peers) // 8) * 8
    slots = peers * cap
    table = jnp.stack([link_neighbor, link_site, link_occupation]).reshape(3, links)
    vmem = pl.BlockSpec(memory_space=pltpu.VMEM)
    state = jax.ShapeDtypeStruct(rho_real.shape, F32)
    return pl.pallas_call(
        functools.partial(kernel, peers, cap, mat_dev, link_count, sites),
        out_shape=(state, state),
        in_specs=[vmem] * 8,
        out_specs=(vmem, vmem),
        scratch_shapes=[
            pltpu.VMEM((4, peers, 4, cap, sites), F32),
            pltpu.VMEM((4, peers, 4, cap, sites), F32),
            pltpu.VMEM((peers, cap, 128), jnp.int32),
            pltpu.VMEM((peers, cap, 128), jnp.int32),
            pltpu.VMEM((sites, sites), F32),
            pltpu.VMEM((mat_dev, 2, sites, sites), F32),
            pltpu.VMEM((mat_dev, 2, sites, sites), F32),
            pltpu.VMEM((slots, 2 * mat_dev * sites), BF16),
            pltpu.VMEM((mat_dev * sites, 2 * slots), BF16),
            pltpu.VMEM((slots, sites), F32),
            pltpu.VMEM((slots, sites), F32),
            pltpu.VMEM((2, 2 * mat_dev * sites, sites), BF16),
            pltpu.VMEM((2, sites, 2 * mat_dev * sites), BF16),
            pltpu.VMEM((4, 2 * slots, sites), BF16),
            pltpu.SemaphoreType.DMA((2,)),
            pltpu.SemaphoreType.DMA((4,)),
            pltpu.SemaphoreType.DMA((4,)),
        ],
        compiler_params=pltpu.CompilerParams(
            collective_id=0, has_side_effects=True, vmem_limit_bytes=60 * 1024 * 1024
        ),
    )(
        rho_real,
        rho_imag,
        hamiltonian,
        damping.reshape(1, sites),
        up_scale.reshape(1, sites),
        bath_real.reshape(1, sites),
        bath_imag.reshape(1, sites),
        table,
    )


def solution(mesh):
    split_3 = P("aux", None, None)
    split_2 = P("aux", None)
    in_specs = (split_3, split_3, P(), P(), P(), P(), P(), split_2, split_2, split_2)
    return jax.shard_map(
        local, mesh=mesh, in_specs=in_specs, out_specs=(split_3, split_3), check_vma=False
    )
```

```python
import functools

import jax
import jax.numpy as jnp
from jax import lax
from jax.experimental import pallas as pl
from jax.experimental.pallas import tpu as pltpu
from jax.sharding import PartitionSpec as P

DOWN = 3
STEP_SIZE = 0.25
MESH = pl.DeviceIdType.MESH
F32 = jnp.float32
BF16 = jnp.bfloat16
NN = (((1,), (0,)), ((), ()))
NT = (((1,), (1,)), ((), ()))


def split(value):
    high = value.astype(BF16)
    return high, (value - high.astype(F32)).astype(BF16)


def dot(a, b, dims=NN):
    return lax.dot_general(a, b, dims, preferred_element_type=F32)


def exact_dot(a, b):
    return jnp.dot(a, b, precision=lax.Precision.HIGHEST, preferred_element_type=F32)


def kernel(
    peers,
    cap,
    mat_dev,
    link_count,
    sites,
    rho_re,
    rho_im,
    ham_in,
    damping,
    up_scale,
    bath_re,
    bath_im,
    table,
    cur_re,
    cur_im,
    send,
    recv,
    req_send,
    req_recv,
    ham,
    acc,
    base,
    pick,
    put,
    coef_re,
    coef_im,
    stack,
    wide,
    terms,
    req_sems,
    send_sems,
    recv_sems,
):
    me = lax.axis_index("aux")
    slots = peers * cap
    links = mat_dev * link_count

    barrier = pltpu.get_barrier_semaphore()

    def greet(k, carry):
        pl.semaphore_signal(
            barrier, inc=1, device_id=(lax.rem(me + k, peers),), device_id_type=MESH
        )
        return carry

    lax.fori_loop(1, peers, greet, 0)

    neighbor = table[0:1, :]
    site = table[1:2, :]
    occupied = table[2:3, :]
    owner = neighbor // mat_dev
    owner_here = jnp.broadcast_to(owner.astype(F32), (links, links))
    owner_there = owner_here.T
    first = lax.broadcasted_iota(jnp.int32, (links, links), 0)
    second = lax.broadcasted_iota(jnp.int32, (links, links), 1)
    earlier = jnp.where((owner_here == owner_there) & (first < second), 1.0, 0.0)
    rank = jnp.sum(earlier, axis=0, keepdims=True).astype(jnp.int32)
    slot = owner * cap + rank
    lane = lax.broadcasted_iota(jnp.int32, (1, links), 1)
    holder = lane // link_count
    upward = (lane - holder * link_count < link_count - DOWN).astype(jnp.int32)
    code = site + sites * (
        (neighbor - owner * mat_dev) + mat_dev * (holder + mat_dev * (upward + 2 * occupied))
    )
    slot_index = lax.broadcasted_iota(jnp.int32, (slots, links), 0)
    code_slot = (
        jnp.sum(
            jnp.where(slot_index == slot, (code + 1).astype(F32), 0.0), axis=1, keepdims=True
        ).astype(jnp.int32)
        - 1
    )
    used = code_slot >= 0
    safe = jnp.maximum(code_slot, 0)
    wanted = jnp.where(used, safe % (sites * mat_dev), -1)
    req_send[...] = jnp.broadcast_to(wanted, (slots, 128)).reshape(peers, cap, 128)

    pl.semaphore_wait(barrier, peers - 1)

    def request(k, carry):
        peer = lax.rem(me + k, peers)
        pltpu.make_async_remote_copy(
            src_ref=req_send.at[peer],
            dst_ref=req_recv.at[me],
            send_sem=req_sems.at[0],
            recv_sem=req_sems.at[1],
            device_id=(peer,),
            device_id_type=MESH,
        ).start()
        return carry

    lax.fori_loop(1, peers, request, 0)
    req_recv[me] = req_send[me]

    site_slot = jnp.where(used, safe % sites, -1)
    rest = safe // (sites * mat_dev)
    holder_slot = jnp.where(used, rest % mat_dev, -1)
    rest = rest // mat_dev
    up_slot = used & (rest % 2 == 1)
    occ_slot = jnp.where(used, (rest // 2).astype(F32), 0.0)
    own_site = lax.broadcasted_iota(jnp.int32, (slots, sites), 1) == site_slot

    def look_up(ref):
        return jnp.sum(jnp.where(own_site, ref[...], 0.0), axis=1, keepdims=True)

    part_re = jnp.where(up_slot, 0.0, occ_slot * look_up(bath_im))
    part_im = jnp.where(up_slot, look_up(up_scale) * jnp.sqrt(occ_slot), occ_slot * look_up(bath_re))
    coef_re[...] = jnp.broadcast_to(part_re, (slots, sites))
    coef_im[...] = jnp.broadcast_to(part_im, (slots, sites))
    rate = jnp.where(up_slot, 0.0, occ_slot * look_up(damping))
    gamma = [
        jnp.sum(jnp.where(holder_slot == m, rate, 0.0), axis=0, keepdims=True)
        for m in range(mat_dev)
    ]
    target = jnp.where(used, holder_slot * sites + site_slot, -1).astype(F32)
    target = jnp.broadcast_to(target, (slots, 128)).T[0:1, :].astype(jnp.int32)
    placed = lax.broadcasted_iota(jnp.int32, (mat_dev * sites, slots), 0) == target
    placed = jnp.where(placed, 1.0, 0.0).astype(BF16)
    put[:, 0:slots] = placed
    put[:, slots:] = placed

    ham[...] = 0.5 * (ham_in[...] + ham_in[...].T)
    cur_re[...] = rho_re[...]
    cur_im[...] = rho_im[...]
    acc[...] = jnp.zeros_like(acc)

    pltpu.make_async_copy(
        req_recv.at[pl.ds(0, peers - 1)], req_recv.at[pl.ds(0, peers - 1)], req_sems.at[1]
    ).wait()
    asked = req_recv[...].reshape(slots, 128)[:, 0:1]
    depth = mat_dev * sites
    picked = lax.broadcasted_iota(jnp.int32, (slots, depth), 1) == asked
    picked = jnp.where(picked, 1.0, 0.0).astype(BF16)
    pick[:, 0:depth] = picked
    pick[:, depth:] = picked

    def stage(t, carry):
        for c, cur in enumerate((cur_re, cur_im)):
            for m in range(mat_dev):
                high, low = split(cur[m])
                stack[c, m * sites : (m + 1) * sites, :] = high
                stack[c, depth + m * sites : depth + (m + 1) * sites, :] = low
                wide[c, :, m * sites : (m + 1) * sites] = high
                wide[c, :, depth + m * sites : depth + (m + 1) * sites] = low
        for c in range(2):
            send[t, :, c] = dot(pick[...], stack[c]).reshape(peers, cap, sites)
            send[t, :, 2 + c] = dot(pick[...], wide[c], NT).reshape(peers, cap, sites)

        def post(k, carry):
            peer = lax.rem(me + k, peers)
            pltpu.make_async_remote_copy(
                src_ref=send.at[t, peer],
                dst_ref=recv.at[t, me],
                send_sem=send_sems.at[t],
                recv_sem=recv_sems.at[t],
                device_id=(peer,),
                device_id_type=MESH,
            ).start()
            return carry

        lax.fori_loop(peers // 2, peers, post, 0)
        lax.fori_loop(1, peers // 2, post, 0)
        recv[t, me] = send[t, me]

        last = t == 3
        weight = jnp.where(last, STEP_SIZE / 6.0, jnp.where(t == 2, STEP_SIZE, 0.5 * STEP_SIZE))
        share = jnp.where(t == 0, -1.0 / 3.0, jnp.where(t == 2, 2.0 / 3.0, 1.0 / 3.0))
        keep = jnp.where(last, 0.0, 1.0)
        for m in range(mat_dev):
            here_re, here_im = cur_re[m], cur_im[m]
            acc_re = acc[m, 0] + share * here_re
            acc_im = acc[m, 1] + share * here_im
            acc[m, 0] = acc_re
            acc[m, 1] = acc_im
            comm_re = exact_dot(ham[...], here_re) - exact_dot(here_re, ham[...])
            comm_im = exact_dot(ham[...], here_im) - exact_dot(here_im, ham[...])
            from_re = jnp.where(last, acc_re, rho_re[m])
            from_im = jnp.where(last, acc_im, rho_im[m])
            base[m, 0] = from_re + weight * (comm_im - gamma[m] * here_re)
            base[m, 1] = from_im - weight * (comm_re + gamma[m] * here_im)

        pltpu.make_async_copy(
            recv.at[t, pl.ds(0, peers - 1)], recv.at[t, pl.ds(0, peers - 1)], recv_sems.at[t]
        ).wait()
        pieces = [recv[t, :, q].reshape(slots, sites) for q in range(4)]
        by_re = weight * coef_re[...]
        by_im = weight * coef_im[...]
        added = []
        for q, term in enumerate(
            (
                by_re * pieces[0] + by_im * pieces[1],
                by_re * pieces[1] - by_im * pieces[0],
                by_re * pieces[2] - by_im * pieces[3],
                by_re * pieces[3] + by_im * pieces[2],
            )
        ):
            high, low = split(term)
            terms[q, 0:slots, :] = high
            terms[q, slots:, :] = low
            added.append(dot(put[...], terms[q]))
        for c, cur in enumerate((cur_re, cur_im)):
            for m in range(mat_dev):
                rows = slice(m * sites, (m + 1) * sites)
                cur[m] = base[m, c] + added[c][rows] + added[2 + c][rows].T
        return carry

    lax.fori_loop(0, 4, stage, 0)

    pltpu.make_async_copy(
        req_send.at[pl.ds(0, peers - 1)], req_send.at[pl.ds(0, peers - 1)], req_sems.at[0]
    ).wait()
    for t in range(4):
        pltpu.make_async_copy(
            send.at[t, pl.ds(0, peers - 1)], send.at[t, pl.ds(0, peers - 1)], send_sems.at[t]
        ).wait()


def run_plain(peers, cap, mat_dev, link_count, sites, arrays):
    slots = peers * cap
    vmem = pl.BlockSpec(memory_space=pltpu.VMEM)
    state = jax.ShapeDtypeStruct((mat_dev, sites, sites), F32)
    return pl.pallas_call(
        functools.partial(kernel, peers, cap, mat_dev, link_count, sites),
        out_shape=(state, state),
        in_specs=[vmem] * 8,
        out_specs=(vmem, vmem),
        scratch_shapes=[
            pltpu.VMEM((4, peers, 4, cap, sites), F32),
            pltpu.VMEM((4, peers, 4, cap, sites), F32),
            pltpu.VMEM((peers, cap, 128), jnp.int32),
            pltpu.VMEM((peers, cap, 128), jnp.int32),
            pltpu.VMEM((sites, sites), F32),
            pltpu.VMEM((mat_dev, 2, sites, sites), F32),
            pltpu.VMEM((mat_dev, 2, sites, sites), F32),
            pltpu.VMEM((slots, 2 * mat_dev * sites), BF16),
            pltpu.VMEM((mat_dev * sites, 2 * slots), BF16),
            pltpu.VMEM((slots, sites), F32),
            pltpu.VMEM((slots, sites), F32),
            pltpu.VMEM((2, 2 * mat_dev * sites, sites), BF16),
            pltpu.VMEM((2, sites, 2 * mat_dev * sites), BF16),
            pltpu.VMEM((4, 2 * slots, sites), BF16),
            pltpu.SemaphoreType.DMA((2,)),
            pltpu.SemaphoreType.DMA((4,)),
            pltpu.SemaphoreType.DMA((4,)),
        ],
        compiler_params=pltpu.CompilerParams(
            collective_id=0, has_side_effects=True, vmem_limit_bytes=60 * 1024 * 1024
        ),
    )(*arrays)


DIRECT = 4
PACKED = 24


def read_tables(peers, mat_dev, table, all_tables, worst, slab, landed, send_sem, recv_sem):
    me = lax.axis_index("aux")
    links = table.shape[1]
    barrier = pltpu.get_barrier_semaphore()

    def greet(k, carry):
        pl.semaphore_signal(
            barrier, inc=1, device_id=(lax.rem(me + k, peers),), device_id_type=MESH
        )
        return carry

    lax.fori_loop(1, peers, greet, 0)
    slab[...] = jnp.zeros_like(slab)
    slab[0:3, :] = table[...]
    pl.semaphore_wait(barrier, peers - 1)

    def post(k, carry):
        peer = lax.rem(me + k, peers)
        pltpu.make_async_remote_copy(
            src_ref=slab,
            dst_ref=landed.at[me],
            send_sem=send_sem,
            recv_sem=recv_sem,
            device_id=(peer,),
            device_id_type=MESH,
        ).start()
        return carry

    lax.fori_loop(1, peers, post, 0)
    landed[me] = slab[...]
    others = landed.at[pl.ds(0, peers - 1)]
    pltpu.make_async_copy(others, others, recv_sem).wait()
    tables = landed[...]
    neighbor = tables[:, 0, :]
    all_tables[0] = neighbor
    all_tables[1] = tables[:, 1, :]
    owner = neighbor // mat_dev
    lane = lax.broadcasted_iota(jnp.int32, (peers, links), 1)
    row = lax.broadcasted_iota(jnp.int32, (peers, links), 0)
    counts = jnp.zeros((peers, links), F32)
    for d in range(peers):
        count = jnp.sum(jnp.where(owner == d, 1.0, 0.0), axis=1, keepdims=True)
        counts = jnp.where(lane == d, count, counts)
    half = peers // 2
    apart = (lane // half) != (row // half)
    over = jnp.where(apart & (lane < peers), jnp.maximum(counts - DIRECT, 0.0), 0.0)
    most = jnp.max(jnp.sum(over, axis=0, keepdims=True), axis=1, keepdims=True)
    worst[...] = jnp.broadcast_to(most, worst.shape).astype(jnp.int32)
    pltpu.make_async_copy(others, others, send_sem).wait()


def packed_kernel(
    peers,
    mat_dev,
    link_count,
    sites,
    rho_re,
    rho_im,
    ham_in,
    damping,
    up_scale,
    bath_re,
    bath_im,
    table,
    all_tables,
    cur_re,
    cur_im,
    send_low,
    send_high,
    send_pack,
    send_relay,
    recv_low,
    recv_high,
    recv_pack,
    ham,
    acc,
    base,
    ask_high,
    spread_all,
    pick,
    spread,
    put,
    coef_re,
    coef_im,
    stack,
    wide,
    terms,
    send_sems,
    recv_sems,
):
    me = lax.axis_index("aux")
    half = peers // 2
    links = mat_dev * link_count
    depth = mat_dev * sites
    block = peers * 8
    slots = 2 * block
    mirror = lax.rem(me + half, peers)
    home = (me // half) * half
    place = me - home
    away = half - home

    barrier = pltpu.get_barrier_semaphore()

    def greet(k, carry):
        pl.semaphore_signal(
            barrier, inc=1, device_id=(lax.rem(me + k, peers),), device_id_type=MESH
        )
        return carry

    lax.fori_loop(1, peers, greet, 0)

    neighbors = all_tables[0]
    wanted_all = ((neighbors % mat_dev) * sites + all_tables[1] + 1).astype(F32)
    first = lax.broadcasted_iota(jnp.int32, (links, links), 0)
    second = lax.broadcasted_iota(jnp.int32, (links, links), 1)
    before = jnp.where(first < second, 1.0, 0.0)
    lane_of = lax.broadcasted_iota(jnp.int32, (peers, links), 1)
    row_of = lax.broadcasted_iota(jnp.int32, (peers, links), 0)

    def asked_of(owner):
        mask = neighbors // mat_dev == owner
        ranks = dot(jnp.where(mask, 1.0, 0.0).astype(BF16), before.astype(BF16))
        out = jnp.zeros((peers, links), F32)
        for k in range(2 * DIRECT):
            found = jnp.sum(
                jnp.where(mask & (ranks == k), wanted_all, 0.0), axis=1, keepdims=True
            )
            out = jnp.where(lane_of == k, found, out)
        return out

    def as_rows(value, start):
        lane = lax.broadcasted_iota(jnp.int32, (peers, 8, links), 2)
        row = lax.broadcasted_iota(jnp.int32, (peers, 8, links), 1)
        spot = jnp.where(lane == start + row % DIRECT, value.reshape(peers, 1, links), 0.0)
        return jnp.sum(spot, axis=2, keepdims=True).reshape(block, 1)

    part = (lax.broadcasted_iota(jnp.int32, (block, 1), 0) // DIRECT) % 2

    def ask_matrix(rows):
        target = jnp.where(rows > 0.5, rows.astype(jnp.int32) - 1 + depth * part, -1)
        match = lax.broadcasted_iota(jnp.int32, (block, 2 * depth), 1) == target
        return jnp.where(match, 1.0, 0.0).astype(BF16)

    earlier_row = lax.broadcasted_iota(jnp.int32, (peers, peers), 0)
    earlier_col = lax.broadcasted_iota(jnp.int32, (peers, peers), 1)
    above = jnp.where(earlier_col < earlier_row, 1.0, 0.0).astype(BF16)

    def packing(asked, group):
        keep = (row_of // half == group) & (lane_of >= DIRECT) & (asked > 0.5)
        flags = jnp.where(keep, 1.0, 0.0)
        rows_before = jnp.sum(dot(above, flags.astype(BF16)), axis=1, keepdims=True)
        position = rows_before + dot(flags.astype(BF16), before.astype(BF16))
        rows = as_rows(jnp.where(keep, position + 1.0, 0.0), DIRECT).astype(jnp.int32)
        target = jnp.where((rows > 0) & (rows <= PACKED), rows - 1 + PACKED * part, -1)
        return lax.broadcasted_iota(jnp.int32, (block, 128), 1) == target

    mine = asked_of(me)
    asked_mirror = asked_of(mirror)
    high_all = ask_matrix(as_rows(mine, DIRECT))
    ask_high[...] = high_all.astype(F32)
    pack = jnp.where(packing(mine, 1 - me // half), 1.0, 0.0).T[0 : 2 * PACKED, :].astype(BF16)
    spread_all[...] = jnp.where(packing(asked_mirror, me // half), 1.0, 0.0)
    pick[0:block, 0 : 2 * depth] = ask_matrix(as_rows(mine, 0))
    pick[block : block + half * 8, 0 : 2 * depth] = ask_high[
        pl.ds(pl.multiple_of(home * 8, 128), half * 8), :
    ].astype(BF16)
    pick[block + half * 8 :, 0 : 2 * depth] = dot(pack, high_all).astype(BF16)
    pick[:, 2 * depth :] = pick[:, 0 : 2 * depth]
    spread[...] = spread_all[pl.ds(pl.multiple_of(home * 8, 128), half * 8), :].astype(BF16)

    neighbor = table[0:1, :]
    owner = neighbor // mat_dev
    owner_here = jnp.broadcast_to(owner.astype(F32), (links, links))
    same = jnp.where((owner_here == owner_here.T) & (first < second), 1.0, 0.0)
    rank = jnp.sum(same, axis=0, keepdims=True).astype(jnp.int32)
    landing = (rank // DIRECT) * block + owner * 8 + rank % DIRECT
    lane = lax.broadcasted_iota(jnp.int32, (1, links), 1)
    holder = lane // link_count
    upward = (lane - holder * link_count < link_count - DOWN).astype(jnp.int32)
    code = table[1:2, :] + sites * (holder + mat_dev * (upward + 2 * table[2:3, :]))
    slot_index = lax.broadcasted_iota(jnp.int32, (slots, links), 0)
    slot_base = slot_index - DIRECT * ((slot_index // DIRECT) % 2)
    code_slot = (
        jnp.sum(
            jnp.where(slot_base == landing, (code + 1).astype(F32), 0.0), axis=1, keepdims=True
        ).astype(jnp.int32)
        - 1
    )
    used = code_slot >= 0
    safe = jnp.maximum(code_slot, 0)
    site_slot = jnp.where(used, safe % sites, -1)
    rest = safe // sites
    holder_slot = jnp.where(used, rest % mat_dev, -1)
    rest = rest // mat_dev
    up_slot = used & (rest % 2 == 1)
    occ_slot = jnp.where(used, (rest // 2).astype(F32), 0.0)
    own_site = lax.broadcasted_iota(jnp.int32, (slots, sites), 1) == site_slot

    def look_up(ref):
        return jnp.sum(jnp.where(own_site, ref[...], 0.0), axis=1, keepdims=True)

    component = (lax.broadcasted_iota(jnp.int32, (slots, 1), 0) // DIRECT) % 2
    part_re = jnp.where(up_slot, 0.0, occ_slot * look_up(bath_im))
    part_im = jnp.where(up_slot, look_up(up_scale) * jnp.sqrt(occ_slot), occ_slot * look_up(bath_re))
    part_im = jnp.where(component == 0, part_im, -part_im)
    coef_re[...] = jnp.broadcast_to(part_re, (slots, sites))
    coef_im[...] = jnp.broadcast_to(part_im, (slots, sites))
    rate = jnp.where(up_slot | (component == 1), 0.0, occ_slot * look_up(damping))
    gamma = [
        jnp.sum(jnp.where(holder_slot == m, rate, 0.0), axis=0, keepdims=True)
        for m in range(mat_dev)
    ]
    target = jnp.where(used, component * depth + holder_slot * sites + site_slot, -1)
    target = jnp.broadcast_to(target.astype(F32), (slots, 128)).T[0:1, :].astype(jnp.int32)
    placed = lax.broadcasted_iota(jnp.int32, (2 * depth, slots), 0) == target
    placed = jnp.where(placed, 1.0, 0.0).astype(BF16)
    put[:, 0:slots] = placed
    put[:, slots:] = placed

    ham[...] = 0.5 * (ham_in[...] + ham_in[...].T)
    cur_re[...] = rho_re[...]
    cur_im[...] = rho_im[...]
    acc[...] = jnp.zeros_like(acc)
    pl.semaphore_wait(barrier, peers - 1)

    def send(source, target, t, kind, peer):
        return pltpu.make_async_remote_copy(
            src_ref=source,
            dst_ref=target,
            send_sem=send_sems.at[t, kind],
            recv_sem=recv_sems.at[t, kind % 3],
            device_id=(peer,),
            device_id_type=MESH,
        )

    def stage(t, carry):
        for c, cur in enumerate((cur_re, cur_im)):
            for m in range(mat_dev):
                high, low = split(cur[m])
                at = c * depth + m * sites
                stack[at : at + sites, :] = high
                stack[2 * depth + at : 2 * depth + at + sites, :] = low
                wide[:, at : at + sites] = high
                wide[:, 2 * depth + at : 2 * depth + at + sites] = low
        for p, pieces in enumerate((dot(pick[...], stack[...]), dot(pick[...], wide[...], NT))):
            send_low[t, :, p] = pieces[0:block].reshape(peers, 8, sites)
            send_high[t, :, p] = pieces[block : block + half * 8].reshape(half, 8, sites)
            send_pack[t, p] = pieces[block + half * 8 :]

        send(send_pack.at[t], recv_pack.at[t], t, 2, mirror).start()

        def across(k, c):
            peer = away + lax.rem(place + k, half)
            send(send_low.at[t, peer], recv_low.at[t, me], t, 0, peer).start()
            return c

        def near(k, c):
            there = lax.rem(place + k, half)
            peer = home + there
            send(send_low.at[t, peer], recv_low.at[t, me], t, 0, peer).start()
            send(send_high.at[t, there], recv_high.at[t, me], t, 1, peer).start()
            return c

        lax.fori_loop(0, half, across, 0)
        lax.fori_loop(1, half, near, 0)
        recv_low[t, me] = send_low[t, me]
        recv_high[t, me] = send_high[t, place]

        last = t == 3
        weight = jnp.where(last, STEP_SIZE / 6.0, jnp.where(t == 2, STEP_SIZE, 0.5 * STEP_SIZE))
        share = jnp.where(t == 0, -1.0 / 3.0, jnp.where(t == 2, 2.0 / 3.0, 1.0 / 3.0))

        def alone(m):
            here_re, here_im = cur_re[m], cur_im[m]
            acc_re = acc[m, 0] + share * here_re
            acc_im = acc[m, 1] + share * here_im
            acc[m, 0] = acc_re
            acc[m, 1] = acc_im
            comm_re = exact_dot(ham[...], here_re) - exact_dot(here_re, ham[...])
            comm_im = exact_dot(ham[...], here_im) - exact_dot(here_im, ham[...])
            from_re = jnp.where(last, acc_re, rho_re[m])
            from_im = jnp.where(last, acc_im, rho_im[m])
            base[m, 0] = from_re + weight * (comm_im - gamma[m] * here_re)
            base[m, 1] = from_im - weight * (comm_re + gamma[m] * here_im)

        for m in range(mat_dev // 2):
            alone(m)

        send(send_pack.at[t], recv_pack.at[t], t, 2, mirror).wait_recv()
        for p in range(2):
            high, low = split(recv_pack[t, p])
            relay = dot(spread[:, 0 : 2 * PACKED], high) + dot(spread[:, 0 : 2 * PACKED], low)
            send_relay[t, :, p] = relay.reshape(half, 8, sites)

        def pass_on(k, c):
            there = lax.rem(place + k, half)
            send(
                send_relay.at[t, there], recv_high.at[t, mirror], t, 4, home + there
            ).start()
            return c

        lax.fori_loop(1, half, pass_on, 0)
        recv_high[t, mirror] = send_relay[t, place]

        for m in range(mat_dev // 2, mat_dev):
            alone(m)

        lows = recv_low.at[t, pl.ds(0, peers - 1)]
        pltpu.make_async_copy(lows, lows, recv_sems.at[t, 0]).wait()
        highs = recv_high.at[t, pl.ds(0, peers - 2)]
        pltpu.make_async_copy(highs, highs, recv_sems.at[t, 1]).wait()
        by_re = weight * coef_re[...]
        by_im = weight * coef_im[...]
        added = []
        for p in range(2):
            whole = jnp.concatenate([recv_low[t, :, p], recv_high[t, :, p]], axis=0)
            turned = pltpu.roll(whole, DIRECT, 1).reshape(slots, sites)
            whole = whole.reshape(slots, sites)
            cross = by_im * turned
            term = by_re * whole + (cross if p == 0 else -cross)
            high, low = split(term)
            terms[p, 0:slots, :] = high
            terms[p, slots:, :] = low
            added.append(dot(put[...], terms[p]))
        for c, cur in enumerate((cur_re, cur_im)):
            for m in range(mat_dev):
                rows = slice(c * depth + m * sites, c * depth + (m + 1) * sites)
                cur[m] = base[m, c] + added[0][rows] + added[1][rows].T
        return carry

    lax.fori_loop(0, 4, stage, 0)

    def drain(t, carry):
        lows = send_low.at[t, pl.ds(0, peers - 1)]
        pltpu.make_async_copy(lows, lows, send_sems.at[t, 0]).wait()
        highs = send_high.at[t, pl.ds(0, half - 1)]
        pltpu.make_async_copy(highs, highs, send_sems.at[t, 1]).wait()
        send(send_pack.at[t], recv_pack.at[t], t, 2, mirror).wait_send()
        relays = send_relay.at[t, pl.ds(0, half - 1)]
        pltpu.make_async_copy(relays, relays, send_sems.at[t, 4]).wait()
        return carry

    lax.fori_loop(0, 4, drain, 0)


def run_packed(peers, mat_dev, link_count, sites, arrays):
    half = peers // 2
    depth = mat_dev * sites
    slots = peers * 16
    rows = peers * 8 + half * 8 + 2 * PACKED
    vmem = pl.BlockSpec(memory_space=pltpu.VMEM)
    state = jax.ShapeDtypeStruct((mat_dev, sites, sites), F32)
    return pl.pallas_call(
        functools.partial(packed_kernel, peers, mat_dev, link_count, sites),
        out_shape=(state, state),
        in_specs=[vmem] * 9,
        out_specs=(vmem, vmem),
        scratch_shapes=[
            pltpu.VMEM((4, peers, 2, 8, sites), F32),
            pltpu.VMEM((4, half, 2, 8, sites), F32),
            pltpu.VMEM((4, 2, 2 * PACKED, sites), F32),
            pltpu.VMEM((4, half, 2, 8, sites), F32),
            pltpu.VMEM((4, peers, 2, 8, sites), F32),
            pltpu.VMEM((4, peers, 2, 8, sites), F32),
            pltpu.VMEM((4, 2, 2 * PACKED, sites), F32),
            pltpu.VMEM((sites, sites), F32),
            pltpu.VMEM((mat_dev, 2, sites, sites), F32),
            pltpu.VMEM((mat_dev, 2, sites, sites), F32),
            pltpu.VMEM((peers * 8, 2 * depth), F32),
            pltpu.VMEM((peers * 8, 128), F32),
            pltpu.VMEM((rows, 4 * depth), BF16),
            pltpu.VMEM((half * 8, 128), BF16),
            pltpu.VMEM((2 * depth, 2 * slots), BF16),
            pltpu.VMEM((slots, sites), F32),
            pltpu.VMEM((slots, sites), F32),
            pltpu.VMEM((4 * depth, sites), BF16),
            pltpu.VMEM((sites, 4 * depth), BF16),
            pltpu.VMEM((2, 2 * slots, sites), BF16),
            pltpu.SemaphoreType.DMA((4, 5)),
            pltpu.SemaphoreType.DMA((4, 3)),
        ],
        compiler_params=pltpu.CompilerParams(
            collective_id=1, has_side_effects=True, vmem_limit_bytes=60 * 1024 * 1024
        ),
    )(*arrays)


def run_tables(peers, mat_dev, table):
    vmem = pl.BlockSpec(memory_space=pltpu.VMEM)
    links = table.shape[1]
    return pl.pallas_call(
        functools.partial(read_tables, peers, mat_dev),
        out_shape=(
            jax.ShapeDtypeStruct((2, peers, links), jnp.int32),
            jax.ShapeDtypeStruct((8, 128), jnp.int32),
        ),
        in_specs=[vmem],
        out_specs=(vmem, vmem),
        scratch_shapes=[
            pltpu.VMEM((8, links), jnp.int32),
            pltpu.VMEM((peers, 8, links), jnp.int32),
            pltpu.SemaphoreType.DMA,
            pltpu.SemaphoreType.DMA,
        ],
        compiler_params=pltpu.CompilerParams(collective_id=2, has_side_effects=True),
    )(table)


def local(
    rho_real,
    rho_imag,
    hamiltonian,
    damping,
    up_scale,
    bath_real,
    bath_imag,
    link_neighbor,
    link_site,
    link_occupation,
):
    peers = lax.axis_size("aux")
    mat_dev, link_count = link_neighbor.shape
    sites = rho_real.shape[1]
    links = mat_dev * link_count
    cap = -(-max(2, 2 * links // peers) // 8) * 8
    table = jnp.stack([link_neighbor, link_site, link_occupation]).reshape(3, links)
    arrays = (
        rho_real,
        rho_imag,
        hamiltonian,
        damping.reshape(1, sites),
        up_scale.reshape(1, sites),
        bath_real.reshape(1, sites),
        bath_imag.reshape(1, sites),
        table,
    )

    def plain(*given):
        return run_plain(peers, cap, mat_dev, link_count, sites, given[:8])

    if peers % 32 or max(2, 2 * links // peers) != 2 * DIRECT or links != 128:
        return plain(*arrays)
    all_tables, worst = run_tables(peers, mat_dev, table)
    return lax.cond(
        worst[0, 0] <= PACKED,
        lambda *given: run_packed(peers, mat_dev, link_count, sites, given),
        plain,
        *arrays,
        all_tables,
    )


def solution(mesh):
    split_3 = P("aux", None, None)
    split_2 = P("aux", None)
    in_specs = (split_3, split_3, P(), P(), P(), P(), P(), split_2, split_2, split_2)
    return jax.shard_map(
        local, mesh=mesh, in_specs=in_specs, out_specs=(split_3, split_3), check_vma=False
    )
```

```python
import functools

import jax
import jax.numpy as jnp
from jax import lax
from jax.experimental import pallas as pl
from jax.experimental.pallas import tpu as pltpu
from jax.sharding import PartitionSpec as P

DOWN = 3
STEP_SIZE = 0.25
MESH = pl.DeviceIdType.MESH
F32 = jnp.float32
BF16 = jnp.bfloat16
NN = (((1,), (0,)), ((), ()))
NT = (((1,), (1,)), ((), ()))


def split(value):
    high = value.astype(BF16)
    return high, (value - high.astype(F32)).astype(BF16)


def dot(a, b, dims=NN):
    return lax.dot_general(a, b, dims, preferred_element_type=F32)


def exact_dot(a, b):
    return jnp.dot(a, b, precision=lax.Precision.HIGHEST, preferred_element_type=F32)


def kernel(
    peers,
    cap,
    mat_dev,
    link_count,
    sites,
    rho_re,
    rho_im,
    ham_in,
    damping,
    up_scale,
    bath_re,
    bath_im,
    table,
    cur_re,
    cur_im,
    send,
    recv,
    req_send,
    req_recv,
    ham,
    acc,
    base,
    pick,
    put,
    coef_re,
    coef_im,
    stack,
    wide,
    terms,
    req_sems,
    send_sems,
    recv_sems,
):
    me = lax.axis_index("aux")
    slots = peers * cap
    links = mat_dev * link_count

    barrier = pltpu.get_barrier_semaphore()

    def greet(k, carry):
        pl.semaphore_signal(
            barrier, inc=1, device_id=(lax.rem(me + k, peers),), device_id_type=MESH
        )
        return carry

    lax.fori_loop(1, peers, greet, 0)

    neighbor = table[0:1, :]
    site = table[1:2, :]
    occupied = table[2:3, :]
    owner = neighbor // mat_dev
    owner_here = jnp.broadcast_to(owner.astype(F32), (links, links))
    owner_there = owner_here.T
    first = lax.broadcasted_iota(jnp.int32, (links, links), 0)
    second = lax.broadcasted_iota(jnp.int32, (links, links), 1)
    earlier = jnp.where((owner_here == owner_there) & (first < second), 1.0, 0.0)
    rank = jnp.sum(earlier, axis=0, keepdims=True).astype(jnp.int32)
    slot = owner * cap + rank
    lane = lax.broadcasted_iota(jnp.int32, (1, links), 1)
    holder = lane // link_count
    upward = (lane - holder * link_count < link_count - DOWN).astype(jnp.int32)
    code = site + sites * (
        (neighbor - owner * mat_dev) + mat_dev * (holder + mat_dev * (upward + 2 * occupied))
    )
    slot_index = lax.broadcasted_iota(jnp.int32, (slots, links), 0)
    code_slot = (
        jnp.sum(
            jnp.where(slot_index == slot, (code + 1).astype(F32), 0.0), axis=1, keepdims=True
        ).astype(jnp.int32)
        - 1
    )
    used = code_slot >= 0
    safe = jnp.maximum(code_slot, 0)
    wanted = jnp.where(used, safe % (sites * mat_dev), -1)
    req_send[...] = jnp.broadcast_to(wanted, (slots, 128)).reshape(peers, cap, 128)

    pl.semaphore_wait(barrier, peers - 1)

    def request(k, carry):
        peer = lax.rem(me + k, peers)
        pltpu.make_async_remote_copy(
            src_ref=req_send.at[peer],
            dst_ref=req_recv.at[me],
            send_sem=req_sems.at[0],
            recv_sem=req_sems.at[1],
            device_id=(peer,),
            device_id_type=MESH,
        ).start()
        return carry

    lax.fori_loop(1, peers, request, 0)
    req_recv[me] = req_send[me]

    site_slot = jnp.where(used, safe % sites, -1)
    rest = safe // (sites * mat_dev)
    holder_slot = jnp.where(used, rest % mat_dev, -1)
    rest = rest // mat_dev
    up_slot = used & (rest % 2 == 1)
    occ_slot = jnp.where(used, (rest // 2).astype(F32), 0.0)
    own_site = lax.broadcasted_iota(jnp.int32, (slots, sites), 1) == site_slot

    def look_up(ref):
        return jnp.sum(jnp.where(own_site, ref[...], 0.0), axis=1, keepdims=True)

    part_re = jnp.where(up_slot, 0.0, occ_slot * look_up(bath_im))
    part_im = jnp.where(up_slot, look_up(up_scale) * jnp.sqrt(occ_slot), occ_slot * look_up(bath_re))
    coef_re[...] = jnp.broadcast_to(part_re, (slots, sites))
    coef_im[...] = jnp.broadcast_to(part_im, (slots, sites))
    rate = jnp.where(up_slot, 0.0, occ_slot * look_up(damping))
    gamma = [
        jnp.sum(jnp.where(holder_slot == m, rate, 0.0), axis=0, keepdims=True)
        for m in range(mat_dev)
    ]
    target = jnp.where(used, holder_slot * sites + site_slot, -1).astype(F32)
    target = jnp.broadcast_to(target, (slots, 128)).T[0:1, :].astype(jnp.int32)
    placed = lax.broadcasted_iota(jnp.int32, (mat_dev * sites, slots), 0) == target
    placed = jnp.where(placed, 1.0, 0.0).astype(BF16)
    put[:, 0:slots] = placed
    put[:, slots:] = placed

    ham[...] = 0.5 * (ham_in[...] + ham_in[...].T)
    cur_re[...] = rho_re[...]
    cur_im[...] = rho_im[...]
    acc[...] = jnp.zeros_like(acc)

    pltpu.make_async_copy(
        req_recv.at[pl.ds(0, peers - 1)], req_recv.at[pl.ds(0, peers - 1)], req_sems.at[1]
    ).wait()
    asked = req_recv[...].reshape(slots, 128)[:, 0:1]
    depth = mat_dev * sites
    picked = lax.broadcasted_iota(jnp.int32, (slots, depth), 1) == asked
    picked = jnp.where(picked, 1.0, 0.0).astype(BF16)
    pick[:, 0:depth] = picked
    pick[:, depth:] = picked

    def stage(t, carry):
        for c, cur in enumerate((cur_re, cur_im)):
            for m in range(mat_dev):
                high, low = split(cur[m])
                stack[c, m * sites : (m + 1) * sites, :] = high
                stack[c, depth + m * sites : depth + (m + 1) * sites, :] = low
                wide[c, :, m * sites : (m + 1) * sites] = high
                wide[c, :, depth + m * sites : depth + (m + 1) * sites] = low
        for c in range(2):
            send[t, :, c] = dot(pick[...], stack[c]).reshape(peers, cap, sites)
            send[t, :, 2 + c] = dot(pick[...], wide[c], NT).reshape(peers, cap, sites)

        def post(k, carry):
            peer = lax.rem(me + k, peers)
            pltpu.make_async_remote_copy(
                src_ref=send.at[t, peer],
                dst_ref=recv.at[t, me],
                send_sem=send_sems.at[t],
                recv_sem=recv_sems.at[t],
                device_id=(peer,),
                device_id_type=MESH,
            ).start()
            return carry

        lax.fori_loop(peers // 2, peers, post, 0)
        lax.fori_loop(1, peers // 2, post, 0)
        recv[t, me] = send[t, me]

        last = t == 3
        weight = jnp.where(last, STEP_SIZE / 6.0, jnp.where(t == 2, STEP_SIZE, 0.5 * STEP_SIZE))
        share = jnp.where(t == 0, -1.0 / 3.0, jnp.where(t == 2, 2.0 / 3.0, 1.0 / 3.0))
        keep = jnp.where(last, 0.0, 1.0)
        for m in range(mat_dev):
            here_re, here_im = cur_re[m], cur_im[m]
            acc_re = acc[m, 0] + share * here_re
            acc_im = acc[m, 1] + share * here_im
            acc[m, 0] = acc_re
            acc[m, 1] = acc_im
            comm_re = exact_dot(ham[...], here_re) - exact_dot(here_re, ham[...])
            comm_im = exact_dot(ham[...], here_im) - exact_dot(here_im, ham[...])
            from_re = jnp.where(last, acc_re, rho_re[m])
            from_im = jnp.where(last, acc_im, rho_im[m])
            base[m, 0] = from_re + weight * (comm_im - gamma[m] * here_re)
            base[m, 1] = from_im - weight * (comm_re + gamma[m] * here_im)

        pltpu.make_async_copy(
            recv.at[t, pl.ds(0, peers - 1)], recv.at[t, pl.ds(0, peers - 1)], recv_sems.at[t]
        ).wait()
        pieces = [recv[t, :, q].reshape(slots, sites) for q in range(4)]
        by_re = weight * coef_re[...]
        by_im = weight * coef_im[...]
        added = []
        for q, term in enumerate(
            (
                by_re * pieces[0] + by_im * pieces[1],
                by_re * pieces[1] - by_im * pieces[0],
                by_re * pieces[2] - by_im * pieces[3],
                by_re * pieces[3] + by_im * pieces[2],
            )
        ):
            high, low = split(term)
            terms[q, 0:slots, :] = high
            terms[q, slots:, :] = low
            added.append(dot(put[...], terms[q]))
        for c, cur in enumerate((cur_re, cur_im)):
            for m in range(mat_dev):
                rows = slice(m * sites, (m + 1) * sites)
                cur[m] = base[m, c] + added[c][rows] + added[2 + c][rows].T
        return carry

    lax.fori_loop(0, 4, stage, 0)

    pltpu.make_async_copy(
        req_send.at[pl.ds(0, peers - 1)], req_send.at[pl.ds(0, peers - 1)], req_sems.at[0]
    ).wait()
    for t in range(4):
        pltpu.make_async_copy(
            send.at[t, pl.ds(0, peers - 1)], send.at[t, pl.ds(0, peers - 1)], send_sems.at[t]
        ).wait()


def run_plain(peers, cap, mat_dev, link_count, sites, arrays):
    slots = peers * cap
    vmem = pl.BlockSpec(memory_space=pltpu.VMEM)
    state = jax.ShapeDtypeStruct((mat_dev, sites, sites), F32)
    return pl.pallas_call(
        functools.partial(kernel, peers, cap, mat_dev, link_count, sites),
        out_shape=(state, state),
        in_specs=[vmem] * 8,
        out_specs=(vmem, vmem),
        scratch_shapes=[
            pltpu.VMEM((4, peers, 4, cap, sites), F32),
            pltpu.VMEM((4, peers, 4, cap, sites), F32),
            pltpu.VMEM((peers, cap, 128), jnp.int32),
            pltpu.VMEM((peers, cap, 128), jnp.int32),
            pltpu.VMEM((sites, sites), F32),
            pltpu.VMEM((mat_dev, 2, sites, sites), F32),
            pltpu.VMEM((mat_dev, 2, sites, sites), F32),
            pltpu.VMEM((slots, 2 * mat_dev * sites), BF16),
            pltpu.VMEM((mat_dev * sites, 2 * slots), BF16),
            pltpu.VMEM((slots, sites), F32),
            pltpu.VMEM((slots, sites), F32),
            pltpu.VMEM((2, 2 * mat_dev * sites, sites), BF16),
            pltpu.VMEM((2, sites, 2 * mat_dev * sites), BF16),
            pltpu.VMEM((4, 2 * slots, sites), BF16),
            pltpu.SemaphoreType.DMA((2,)),
            pltpu.SemaphoreType.DMA((4,)),
            pltpu.SemaphoreType.DMA((4,)),
        ],
        compiler_params=pltpu.CompilerParams(
            collective_id=0, has_side_effects=True, vmem_limit_bytes=60 * 1024 * 1024
        ),
    )(*arrays)


DIRECT = 4
PACKED = 24


def read_tables(peers, mat_dev, table, all_tables, worst, slab, landed, send_sem, recv_sem):
    me = lax.axis_index("aux")
    links = table.shape[1]
    barrier = pltpu.get_barrier_semaphore()

    def greet(k, carry):
        pl.semaphore_signal(
            barrier, inc=1, device_id=(lax.rem(me + k, peers),), device_id_type=MESH
        )
        return carry

    lax.fori_loop(1, peers, greet, 0)
    slab[...] = jnp.zeros_like(slab)
    slab[0:3, :] = table[...]
    pl.semaphore_wait(barrier, peers - 1)

    def post(k, carry):
        peer = lax.rem(me + k, peers)
        pltpu.make_async_remote_copy(
            src_ref=slab,
            dst_ref=landed.at[me],
            send_sem=send_sem,
            recv_sem=recv_sem,
            device_id=(peer,),
            device_id_type=MESH,
        ).start()
        return carry

    lax.fori_loop(1, peers, post, 0)
    landed[me] = slab[...]
    others = landed.at[pl.ds(0, peers - 1)]
    pltpu.make_async_copy(others, others, recv_sem).wait()
    tables = landed[...]
    neighbor = tables[:, 0, :]
    all_tables[0] = neighbor
    all_tables[1] = tables[:, 1, :]
    owner = neighbor // mat_dev
    lane = lax.broadcasted_iota(jnp.int32, (peers, links), 1)
    row = lax.broadcasted_iota(jnp.int32, (peers, links), 0)
    counts = jnp.zeros((peers, links), F32)
    for d in range(peers):
        count = jnp.sum(jnp.where(owner == d, 1.0, 0.0), axis=1, keepdims=True)
        counts = jnp.where(lane == d, count, counts)
    half = peers // 2
    apart = (lane // half) != (row // half)
    over = jnp.where(apart & (lane < peers), jnp.maximum(counts - DIRECT, 0.0), 0.0)
    most = jnp.max(jnp.sum(over, axis=0, keepdims=True), axis=1, keepdims=True)
    worst[...] = jnp.broadcast_to(most, worst.shape).astype(jnp.int32)
    pltpu.make_async_copy(others, others, send_sem).wait()


def packed_kernel(
    peers,
    mat_dev,
    link_count,
    sites,
    rho_re,
    rho_im,
    ham_in,
    damping,
    up_scale,
    bath_re,
    bath_im,
    table,
    all_tables,
    cur_re,
    cur_im,
    send_low,
    send_high,
    send_pack,
    send_relay,
    recv_low,
    recv_high,
    recv_pack,
    ham,
    acc,
    base,
    ask_part,
    spread_all,
    gammas,
    pick,
    spread,
    put,
    coef_re,
    coef_im,
    stack,
    wide,
    terms,
    send_sems,
    recv_sems,
):
    me = lax.axis_index("aux")
    half = peers // 2
    links = mat_dev * link_count
    depth = mat_dev * sites
    block = peers * 8
    slots = 2 * block
    mirror = lax.rem(me + half, peers)
    home = (me // half) * half
    place = me - home
    away = half - home

    barrier = pltpu.get_barrier_semaphore()

    def greet(k, carry):
        pl.semaphore_signal(
            barrier, inc=1, device_id=(lax.rem(me + k, peers),), device_id_type=MESH
        )
        return carry

    lax.fori_loop(1, peers, greet, 0)

    neighbors = all_tables[0]
    wanted_all = ((neighbors % mat_dev) * sites + all_tables[1] + 1).astype(F32)
    first = lax.broadcasted_iota(jnp.int32, (links, links), 0)
    second = lax.broadcasted_iota(jnp.int32, (links, links), 1)
    before = jnp.where(first < second, 1.0, 0.0)
    lane_of = lax.broadcasted_iota(jnp.int32, (peers, links), 1)
    row_of = lax.broadcasted_iota(jnp.int32, (peers, links), 0)

    def asked_of(owner):
        mask = neighbors // mat_dev == owner
        ranks = dot(jnp.where(mask, 1.0, 0.0).astype(BF16), before.astype(BF16))
        out = jnp.zeros((peers, links), F32)
        for k in range(2 * DIRECT):
            found = jnp.sum(
                jnp.where(mask & (ranks == k), wanted_all, 0.0), axis=1, keepdims=True
            )
            out = jnp.where(lane_of == k, found, out)
        return out

    def as_rows(value, start):
        lane = lax.broadcasted_iota(jnp.int32, (peers, 8, links), 2)
        row = lax.broadcasted_iota(jnp.int32, (peers, 8, links), 1)
        spot = jnp.where(lane == start + row % DIRECT, value.reshape(peers, 1, links), 0.0)
        return jnp.sum(spot, axis=2, keepdims=True).reshape(block, 1)

    part = (lax.broadcasted_iota(jnp.int32, (block, 1), 0) // DIRECT) % 2

    def ask_matrix(rows):
        target = jnp.where(rows > 0.5, rows.astype(jnp.int32) - 1 + depth * part, -1)
        match = lax.broadcasted_iota(jnp.int32, (block, 2 * depth), 1) == target
        return jnp.where(match, 1.0, 0.0).astype(BF16)

    earlier_row = lax.broadcasted_iota(jnp.int32, (peers, peers), 0)
    earlier_col = lax.broadcasted_iota(jnp.int32, (peers, peers), 1)
    above = jnp.where(earlier_col < earlier_row, 1.0, 0.0).astype(BF16)

    def packing(asked, group):
        keep = (row_of // half == group) & (lane_of >= DIRECT) & (asked > 0.5)
        flags = jnp.where(keep, 1.0, 0.0)
        rows_before = jnp.sum(dot(above, flags.astype(BF16)), axis=1, keepdims=True)
        position = rows_before + dot(flags.astype(BF16), before.astype(BF16))
        rows = as_rows(jnp.where(keep, position + 1.0, 0.0), DIRECT).astype(jnp.int32)
        target = jnp.where((rows > 0) & (rows <= PACKED), rows - 1 + PACKED * part, -1)
        return lax.broadcasted_iota(jnp.int32, (block, 128), 1) == target

    mine = asked_of(me)
    side = half * 8
    far = slice(0, side)
    packed = slice(side, side + 2 * PACKED)
    close = slice(side + 2 * PACKED, 2 * side + 2 * PACKED)
    extra = slice(2 * side + 2 * PACKED, 3 * side + 2 * PACKED)
    ask_low = ask_matrix(as_rows(mine, 0))
    ask_part[...] = ask_low.astype(F32)
    home_rows = pl.ds(pl.multiple_of(home * 8, 128), side)
    pick[far, 0 : 2 * depth] = ask_part[pl.ds(pl.multiple_of(away * 8, 128), side), :].astype(BF16)
    pick[close, 0 : 2 * depth] = ask_part[home_rows, :].astype(BF16)
    ask_high = ask_matrix(as_rows(mine, DIRECT))
    ask_part[...] = ask_high.astype(F32)
    pack = jnp.where(packing(mine, 1 - me // half), 1.0, 0.0).T[0 : 2 * PACKED, :].astype(BF16)
    pick[packed, 0 : 2 * depth] = dot(pack, ask_high).astype(BF16)
    pick[extra, 0 : 2 * depth] = ask_part[home_rows, :].astype(BF16)
    pick[:, 2 * depth :] = pick[:, 0 : 2 * depth]

    def settle():
        asked_mirror = asked_of(mirror)
        spread_all[...] = jnp.where(packing(asked_mirror, me // half), 1.0, 0.0)
        spread[...] = spread_all[home_rows, :].astype(BF16)
        ham[...] = 0.5 * (ham_in[...] + ham_in[...].T)
        acc[...] = jnp.zeros_like(acc)

        neighbor = table[0:1, :]
        owner = neighbor // mat_dev
        owner_here = jnp.broadcast_to(owner.astype(F32), (links, links))
        same = jnp.where((owner_here == owner_here.T) & (first < second), 1.0, 0.0)
        rank = jnp.sum(same, axis=0, keepdims=True).astype(jnp.int32)
        landing = (rank // DIRECT) * block + owner * 8 + rank % DIRECT
        lane = lax.broadcasted_iota(jnp.int32, (1, links), 1)
        holder = lane // link_count
        upward = (lane - holder * link_count < link_count - DOWN).astype(jnp.int32)
        code = table[1:2, :] + sites * (holder + mat_dev * (upward + 2 * table[2:3, :]))
        slot_index = lax.broadcasted_iota(jnp.int32, (slots, links), 0)
        slot_base = slot_index - DIRECT * ((slot_index // DIRECT) % 2)
        code_slot = (
            jnp.sum(
                jnp.where(slot_base == landing, (code + 1).astype(F32), 0.0), axis=1, keepdims=True
            ).astype(jnp.int32)
            - 1
        )
        used = code_slot >= 0
        safe = jnp.maximum(code_slot, 0)
        site_slot = jnp.where(used, safe % sites, -1)
        rest = safe // sites
        holder_slot = jnp.where(used, rest % mat_dev, -1)
        rest = rest // mat_dev
        up_slot = used & (rest % 2 == 1)
        occ_slot = jnp.where(used, (rest // 2).astype(F32), 0.0)
        own_site = lax.broadcasted_iota(jnp.int32, (slots, sites), 1) == site_slot

        def look_up(ref):
            return jnp.sum(jnp.where(own_site, ref[...], 0.0), axis=1, keepdims=True)

        component = (lax.broadcasted_iota(jnp.int32, (slots, 1), 0) // DIRECT) % 2
        part_re = jnp.where(up_slot, 0.0, occ_slot * look_up(bath_im))
        part_im = jnp.where(up_slot, look_up(up_scale) * jnp.sqrt(occ_slot), occ_slot * look_up(bath_re))
        part_im = jnp.where(component == 0, part_im, -part_im)
        coef_re[...] = jnp.broadcast_to(part_re, (slots, sites))
        coef_im[...] = jnp.broadcast_to(part_im, (slots, sites))
        rate = jnp.where(up_slot | (component == 1), 0.0, occ_slot * look_up(damping))
        gamma = [
            jnp.sum(jnp.where(holder_slot == m, rate, 0.0), axis=0, keepdims=True)
            for m in range(mat_dev)
        ]
        target = jnp.where(used, component * depth + holder_slot * sites + site_slot, -1)
        target = jnp.broadcast_to(target.astype(F32), (slots, 128)).T[0:1, :].astype(jnp.int32)
        placed = lax.broadcasted_iota(jnp.int32, (2 * depth, slots), 0) == target
        placed = jnp.where(placed, 1.0, 0.0).astype(BF16)
        put[:, 0:slots] = placed
        put[:, slots:] = placed
        for m in range(mat_dev):
            gammas[m] = jnp.broadcast_to(gamma[m], (8, 128))

    cur_re[...] = rho_re[...]
    cur_im[...] = rho_im[...]
    pl.semaphore_wait(barrier, peers - 1)

    def send(source, target, t, kind, peer):
        return pltpu.make_async_remote_copy(
            src_ref=source,
            dst_ref=target,
            send_sem=send_sems.at[t, kind],
            recv_sem=recv_sems.at[t, kind % 3],
            device_id=(peer,),
            device_id_type=MESH,
        )

    def stage(t, carry):
        for c, cur in enumerate((cur_re, cur_im)):
            for m in range(mat_dev):
                high, low = split(cur[m])
                at = c * depth + m * sites
                stack[at : at + sites, :] = high
                stack[2 * depth + at : 2 * depth + at + sites, :] = low
                wide[:, at : at + sites] = high
                wide[:, 2 * depth + at : 2 * depth + at + sites] = low
        for p in range(2):
            rows = slice(0, side + 2 * PACKED)
            pieces = dot(pick[rows], wide[...], NT) if p else dot(pick[rows], stack[...])
            send_low[t, pl.ds(away, half), p] = pieces[0:side].reshape(half, 8, sites)
            send_pack[t, p] = pieces[side:]

        send(send_pack.at[t], recv_pack.at[t], t, 2, mirror).start()

        def across(k, c):
            peer = away + lax.rem(place + k, half)
            send(send_low.at[t, peer], recv_low.at[t, me], t, 0, peer).start()
            return c

        def near(k, c):
            there = lax.rem(place + k, half)
            peer = home + there
            send(send_low.at[t, peer], recv_low.at[t, me], t, 0, peer).start()
            send(send_high.at[t, there], recv_high.at[t, me], t, 1, peer).start()
            return c

        lax.fori_loop(0, half, across, 0)
        for p in range(2):
            rows = slice(side + 2 * PACKED, 3 * side + 2 * PACKED)
            pieces = dot(pick[rows], wide[...], NT) if p else dot(pick[rows], stack[...])
            send_low[t, pl.ds(home, half), p] = pieces[0:side].reshape(half, 8, sites)
            send_high[t, :, p] = pieces[side:].reshape(half, 8, sites)
        lax.fori_loop(1, half, near, 0)
        recv_low[t, me] = send_low[t, me]
        recv_high[t, me] = send_high[t, place]
        pl.when(t == 0)(settle)

        last = t == 3
        weight = jnp.where(last, STEP_SIZE / 6.0, jnp.where(t == 2, STEP_SIZE, 0.5 * STEP_SIZE))
        share = jnp.where(t == 0, -1.0 / 3.0, jnp.where(t == 2, 2.0 / 3.0, 1.0 / 3.0))

        def alone(m):
            here_re, here_im = cur_re[m], cur_im[m]
            acc_re = acc[m, 0] + share * here_re
            acc_im = acc[m, 1] + share * here_im
            acc[m, 0] = acc_re
            acc[m, 1] = acc_im
            comm_re = exact_dot(ham[...], here_re) - exact_dot(here_re, ham[...])
            comm_im = exact_dot(ham[...], here_im) - exact_dot(here_im, ham[...])
            from_re = jnp.where(last, acc_re, rho_re[m])
            from_im = jnp.where(last, acc_im, rho_im[m])
            gamma = gammas[m][0:1, 0:1]
            base[m, 0] = from_re + weight * (comm_im - gamma * here_re)
            base[m, 1] = from_im - weight * (comm_re + gamma * here_im)

        for m in range(mat_dev // 2):
            alone(m)

        send(send_pack.at[t], recv_pack.at[t], t, 2, mirror).wait_recv()
        for p in range(2):
            high, low = split(recv_pack[t, p])
            relay = dot(spread[:, 0 : 2 * PACKED], high) + dot(spread[:, 0 : 2 * PACKED], low)
            send_relay[t, :, p] = relay.reshape(half, 8, sites)

        def pass_on(k, c):
            there = lax.rem(place + k, half)
            send(
                send_relay.at[t, there], recv_high.at[t, mirror], t, 4, home + there
            ).start()
            return c

        lax.fori_loop(1, half, pass_on, 0)
        recv_high[t, mirror] = send_relay[t, place]

        for m in range(mat_dev // 2, mat_dev):
            alone(m)

        lows = recv_low.at[t, pl.ds(0, peers - 1)]
        pltpu.make_async_copy(lows, lows, recv_sems.at[t, 0]).wait()
        highs = recv_high.at[t, pl.ds(0, peers - 2)]
        pltpu.make_async_copy(highs, highs, recv_sems.at[t, 1]).wait()
        by_re = weight * coef_re[...]
        by_im = weight * coef_im[...]
        added = []
        for p in range(2):
            whole = jnp.concatenate([recv_low[t, :, p], recv_high[t, :, p]], axis=0)
            turned = pltpu.roll(whole, DIRECT, 1).reshape(slots, sites)
            whole = whole.reshape(slots, sites)
            cross = by_im * turned
            term = by_re * whole + (cross if p == 0 else -cross)
            high, low = split(term)
            terms[p, 0:slots, :] = high
            terms[p, slots:, :] = low
            added.append(dot(put[...], terms[p]))
        for c, cur in enumerate((cur_re, cur_im)):
            for m in range(mat_dev):
                rows = slice(c * depth + m * sites, c * depth + (m + 1) * sites)
                cur[m] = base[m, c] + added[0][rows] + added[1][rows].T
        return carry

    lax.fori_loop(0, 4, stage, 0)

    def drain(t, carry):
        lows = send_low.at[t, pl.ds(0, peers - 1)]
        pltpu.make_async_copy(lows, lows, send_sems.at[t, 0]).wait()
        highs = send_high.at[t, pl.ds(0, half - 1)]
        pltpu.make_async_copy(highs, highs, send_sems.at[t, 1]).wait()
        send(send_pack.at[t], recv_pack.at[t], t, 2, mirror).wait_send()
        relays = send_relay.at[t, pl.ds(0, half - 1)]
        pltpu.make_async_copy(relays, relays, send_sems.at[t, 4]).wait()
        return carry

    lax.fori_loop(0, 4, drain, 0)


def run_packed(peers, mat_dev, link_count, sites, arrays):
    half = peers // 2
    depth = mat_dev * sites
    slots = peers * 16
    rows = peers * 8 + half * 8 + 2 * PACKED
    vmem = pl.BlockSpec(memory_space=pltpu.VMEM)
    state = jax.ShapeDtypeStruct((mat_dev, sites, sites), F32)
    return pl.pallas_call(
        functools.partial(packed_kernel, peers, mat_dev, link_count, sites),
        out_shape=(state, state),
        in_specs=[vmem] * 9,
        out_specs=(vmem, vmem),
        scratch_shapes=[
            pltpu.VMEM((4, peers, 2, 8, sites), F32),
            pltpu.VMEM((4, half, 2, 8, sites), F32),
            pltpu.VMEM((4, 2, 2 * PACKED, sites), F32),
            pltpu.VMEM((4, half, 2, 8, sites), F32),
            pltpu.VMEM((4, peers, 2, 8, sites), F32),
            pltpu.VMEM((4, peers, 2, 8, sites), F32),
            pltpu.VMEM((4, 2, 2 * PACKED, sites), F32),
            pltpu.VMEM((sites, sites), F32),
            pltpu.VMEM((mat_dev, 2, sites, sites), F32),
            pltpu.VMEM((mat_dev, 2, sites, sites), F32),
            pltpu.VMEM((peers * 8, 2 * depth), F32),
            pltpu.VMEM((peers * 8, 128), F32),
            pltpu.VMEM((mat_dev, 8, 128), F32),
            pltpu.VMEM((rows, 4 * depth), BF16),
            pltpu.VMEM((half * 8, 128), BF16),
            pltpu.VMEM((2 * depth, 2 * slots), BF16),
            pltpu.VMEM((slots, sites), F32),
            pltpu.VMEM((slots, sites), F32),
            pltpu.VMEM((4 * depth, sites), BF16),
            pltpu.VMEM((sites, 4 * depth), BF16),
            pltpu.VMEM((2, 2 * slots, sites), BF16),
            pltpu.SemaphoreType.DMA((4, 5)),
            pltpu.SemaphoreType.DMA((4, 3)),
        ],
        compiler_params=pltpu.CompilerParams(
            collective_id=1, has_side_effects=True, vmem_limit_bytes=60 * 1024 * 1024
        ),
    )(*arrays)


def run_tables(peers, mat_dev, table):
    vmem = pl.BlockSpec(memory_space=pltpu.VMEM)
    links = table.shape[1]
    return pl.pallas_call(
        functools.partial(read_tables, peers, mat_dev),
        out_shape=(
            jax.ShapeDtypeStruct((2, peers, links), jnp.int32),
            jax.ShapeDtypeStruct((8, 128), jnp.int32),
        ),
        in_specs=[vmem],
        out_specs=(vmem, vmem),
        scratch_shapes=[
            pltpu.VMEM((8, links), jnp.int32),
            pltpu.VMEM((peers, 8, links), jnp.int32),
            pltpu.SemaphoreType.DMA,
            pltpu.SemaphoreType.DMA,
        ],
        compiler_params=pltpu.CompilerParams(collective_id=2, has_side_effects=True),
    )(table)


def local(
    rho_real,
    rho_imag,
    hamiltonian,
    damping,
    up_scale,
    bath_real,
    bath_imag,
    link_neighbor,
    link_site,
    link_occupation,
):
    peers = lax.axis_size("aux")
    mat_dev, link_count = link_neighbor.shape
    sites = rho_real.shape[1]
    links = mat_dev * link_count
    cap = -(-max(2, 2 * links // peers) // 8) * 8
    table = jnp.stack([link_neighbor, link_site, link_occupation]).reshape(3, links)
    arrays = (
        rho_real,
        rho_imag,
        hamiltonian,
        damping.reshape(1, sites),
        up_scale.reshape(1, sites),
        bath_real.reshape(1, sites),
        bath_imag.reshape(1, sites),
        table,
    )

    def plain(*given):
        return run_plain(peers, cap, mat_dev, link_count, sites, given[:8])

    if peers % 32 or max(2, 2 * links // peers) != 2 * DIRECT or links != 128:
        return plain(*arrays)
    all_tables, worst = run_tables(peers, mat_dev, table)
    return lax.cond(
        worst[0, 0] <= PACKED,
        lambda *given: run_packed(peers, mat_dev, link_count, sites, given),
        plain,
        *arrays,
        all_tables,
    )


def solution(mesh):
    split_3 = P("aux", None, None)
    split_2 = P("aux", None)
    in_specs = (split_3, split_3, P(), P(), P(), P(), P(), split_2, split_2, split_2)
    return jax.shard_map(
        local, mesh=mesh, in_specs=in_specs, out_specs=(split_3, split_3), check_vma=False
    )
```
